128 devices in a mesh: grp: 4 (over x), dev: 32 (over z, y, core).
Axes of the slice: x: 4, y: 4, z: 4, core: 2. Of those that a mesh axis runs over, the one named last changes fastest.
Arguments:
- tokens: bfloat16 [131072, 3584], P(('grp', 'dev')), may hold values from -160 to 160
- input_norm_gain: bfloat16 [3584], replicated, may hold values from 0.5 to 1.5
- base_query_value_weight: bfloat16 [3584, 2304], P('grp'), may hold values from -0.09375 to 0.09375
- adapter_down_weight: bfloat16 [128, 3584, 128], P('dev'), may hold values from -0.09375 to 0.09375
- adapter_up_query: bfloat16 [128, 64, 1792], P('dev'), may hold values from -0.75 to 0.75
- adapter_up_value: bfloat16 [128, 64, 512], P('dev'), may hold values from -0.75 to 0.75
- token_adapter_id: int32 [131072, 1], P(('grp', 'dev')), may hold values from 0 to 127, as said below
- adapter_storage_row: int32 [128], replicated, may hold values from 0 to 127, as said below
Outputs:
- adapted_query_output: bfloat16 [131072, 1792], P(('grp', 'dev'))
- adapted_value_output: bfloat16 [131072, 512], P(('grp', 'dev'))
The draws below stay inside these ranges and needn't reach their ends.
Inputs may be any that keep to these rules, and one draw needn't show every extreme that they name: `token_adapter_id`: no adapter is named by more than 16 of the rows of one device, and in every device's rows one adapter is named exactly 16 times. Adapters whose storage rows lie on one index of dev (rows k * 4 to k * 4 + 3) are named by at most 48 of the rows of one device, and exactly 48 times for some index in every device's rows. A permutation: the adapter with id a is row adapter_storage_row[a] of adapter_down_weight, adapter_up_query and adapter_up_value.
All inputs are finite; a program needn't handle non-finite values.
Results may differ from the reference program's by a relative error of at most 0.0054.
Values may be sent and summed in bfloat16 or wider, within the bound.
No kernel may reach another device: no remote copies, remote signals or barrier semaphores. Data moves between devices by JAX's collectives and lax.ppermute only.
A program may use at most 256 MiB of HBM per device.

```python
import math
import jax
import jax.numpy as jnp
from jax import lax

MODEL_WIDTH = 3584
QUERY_WIDTH = 1792
VALUE_WIDTH = 512
ADAPTER_RANK = 64
ADP_DEV = 4
TOK_DEV = 1024
ADAPTER_POOL = 128
CAP = 16
DCAP = 48
TOKENS = 131072
N_DEV = 32


def draw_tokens(key, part):
    key = jax.random.fold_in(key, 11)
    row_key, col_key, val_key = jax.random.split(key, 3)
    row_scale = jnp.exp(jax.random.uniform(row_key, (TOKENS, 1), jnp.float32, 0.0, math.log(10.0)))
    col_scale = jnp.exp(jax.random.uniform(col_key, (1, MODEL_WIDTH), jnp.float32, -math.log(3.0), math.log(3.0)))
    values = jnp.clip(jax.random.normal(val_key, (TOKENS, MODEL_WIDTH), jnp.float32), -5.0, 5.0)
    return (values * row_scale * col_scale).astype(jnp.bfloat16)


def shared_slots(key):
    return jax.random.permutation(jax.random.fold_in(key, 101), ADAPTER_POOL).astype(jnp.int32)


def draw_adapter_storage_row(key, part):
    return shared_slots(key)


def draw_token_adapter_id(key, part):
    slots = shared_slots(key)
    key = jax.random.fold_in(key, 7)
    id_at_slot = jnp.argsort(slots).astype(jnp.int32)
    per_dest = ADP_DEV * CAP
    entries = jnp.arange(ADAPTER_POOL * CAP, dtype=jnp.int32)
    entry_slot = entries // CAP
    entry_dest = entry_slot // ADP_DEV
    blocks = TOKENS // TOK_DEV

    def one_block(block_key):
        heat_key, noise_key, dest_key, local_key, order_key = jax.random.split(block_key, 5)
        heat = jax.random.randint(heat_key, (ADAPTER_POOL,), 0, 4, jnp.int32)
        noise = jax.random.randint(noise_key, (ADAPTER_POOL * CAP,), 0, 1024, jnp.int32)
        full_dest = jax.random.randint(dest_key, (), 0, N_DEV, jnp.int32)
        full_local = jax.random.randint(local_key, (), 0, ADP_DEV, jnp.int32)
        forced = full_dest * ADP_DEV + full_local
        score = heat[entry_slot] * 1024 + noise
        score = jnp.where(entry_slot == forced, 8192, score)
        distinct = score * (ADAPTER_POOL * CAP) + entries
        grid = distinct.reshape(N_DEV, per_dest)
        ordering = jnp.argsort(-grid, axis=1)
        ranking = jnp.argsort(ordering, axis=1).reshape(ADAPTER_POOL * CAP)
        keeper = ranking < DCAP
        lifted = distinct + jnp.where(entry_dest == full_dest, 2 ** 26, 0)
        priority = jnp.where(keeper, lifted, -1 - entries)
        picked = lax.top_k(priority, TOK_DEV)[1]
        picked_slots = entry_slot[picked]
        picked_slots = jax.random.permutation(order_key, picked_slots)
        return id_at_slot[picked_slots]
    keys = jax.random.split(key, blocks)
    return jax.vmap(one_block)(keys).reshape(TOKENS, 1).astype(jnp.int32)


def level_of(own_key, extent, cuts, low, largest):
    def one(axis_at, shards_of):
        draws = jax.random.uniform(jax.random.fold_in(jax.random.fold_in(own_key, 6), axis_at), (shards_of,), jnp.float32, low / len(cuts), largest / len(cuts))
        return jnp.repeat(jnp.exp(draws), extent[axis_at] // shards_of).reshape((-1,) + (1,) * (len(extent) - axis_at - 1))

    gain = one(*cuts[0])
    for cut in cuts[1:]:
        gain = gain * one(*cut)
    return gain


def scatter_about(key, dims, deviation, bound, pieces=(), kind=jnp.bfloat16):
    gain = level_of(key, dims, pieces, -0.22, 0.18) if pieces else 1.0
    result = jax.random.normal(key, dims, jnp.float32) * deviation * gain
    return jnp.minimum(jnp.maximum(result, -bound), bound).astype(kind)


def setup_inputs(seed: int = 0) -> dict:
    arg_keys = jax.random.split(jax.random.key(seed), 9)
    tokens = draw_tokens(jax.random.fold_in(arg_keys[8], 71), 0)
    input_norm_gain = jnp.clip(1.0 + 0.1 * jax.random.normal(arg_keys[1], (MODEL_WIDTH,), jnp.float32), 0.5, 1.5).astype(jnp.bfloat16)
    base_query_value_weight = scatter_about(arg_keys[2], (MODEL_WIDTH, QUERY_WIDTH + VALUE_WIDTH), MODEL_WIDTH ** -0.5, 0.09375, ((0, 4),))
    adapter_down_weight = scatter_about(arg_keys[3], (ADAPTER_POOL, MODEL_WIDTH, 2 * ADAPTER_RANK), MODEL_WIDTH ** -0.5, 0.09375, ((0, 32),))
    adapter_up_query = scatter_about(arg_keys[4], (ADAPTER_POOL, ADAPTER_RANK, QUERY_WIDTH), ADAPTER_RANK ** -0.5, 0.75, ((0, 32),))
    adapter_up_value = scatter_about(arg_keys[5], (ADAPTER_POOL, ADAPTER_RANK, VALUE_WIDTH), ADAPTER_RANK ** -0.5, 0.75, ((0, 32),))
    token_adapter_id = draw_token_adapter_id(jax.random.fold_in(arg_keys[8], 71), 0)
    adapter_storage_row = draw_adapter_storage_row(jax.random.fold_in(arg_keys[8], 71), 0)
    return {"tokens": tokens, "input_norm_gain": input_norm_gain, "base_query_value_weight": base_query_value_weight, "adapter_down_weight": adapter_down_weight, "adapter_up_query": adapter_up_query, "adapter_up_value": adapter_up_value, "token_adapter_id": token_adapter_id, "adapter_storage_row": adapter_storage_row}


adapter_scale = 0.5

def normalize(tokens, input_norm_gain):
    values = tokens.astype(jnp.float32)
    factor = lax.rsqrt(lax.optimization_barrier(jnp.mean(values * values, axis=1, keepdims=True)) + 1e-06)
    return (values * factor * input_norm_gain.astype(jnp.float32)[None, :]).astype(jnp.bfloat16)

def reference(tokens, input_norm_gain, base_query_value_weight, adapter_down_weight, adapter_up_query, adapter_up_value, token_adapter_id, adapter_storage_row):
    slot_of = adapter_storage_row[token_adapter_id[:, 0]].astype(jnp.int32)
    downward_gathered = adapter_down_weight.astype(jnp.float32)
    upward_query_gathered = adapter_up_query.astype(jnp.float32)
    upward_value_gathered = adapter_up_value.astype(jnp.float32)
    catalog = jnp.arange(ADAPTER_POOL, dtype=jnp.int32)
    blocks = TOKENS // TOK_DEV

    def one_block(pair):
        chosen, slot_here = pair
        normed = normalize(chosen, input_norm_gain)
        base_product = jnp.dot(normed, base_query_value_weight, preferred_element_type=jnp.float32)
        onehot = (slot_here[:, None] == catalog[None, :]).astype(jnp.int32)
        before = jnp.cumsum(onehot, axis=0) - onehot
        position = lax.optimization_barrier(jnp.sum(onehot * before, axis=1)).astype(jnp.int32)
        target = (slot_here * CAP + position).astype(jnp.int32)
        buffer = jnp.zeros((ADAPTER_POOL * CAP, MODEL_WIDTH), jnp.bfloat16).at[target].set(normed)
        buffer = buffer.reshape(ADAPTER_POOL, CAP, MODEL_WIDTH)
        reduced_rank_state = jnp.einsum('acd,adr->acr', buffer.astype(jnp.float32), downward_gathered).astype(jnp.bfloat16)
        low_wide = reduced_rank_state.astype(jnp.float32)
        delta_q = jnp.einsum('acr,arq->acq', low_wide[:, :, :ADAPTER_RANK], upward_query_gathered).astype(jnp.bfloat16)
        delta_v = jnp.einsum('acr,arq->acq', low_wide[:, :, ADAPTER_RANK:], upward_value_gathered).astype(jnp.bfloat16)
        query_rank_rows = delta_q.reshape(ADAPTER_POOL * CAP, QUERY_WIDTH)[target]
        value_rank_rows = delta_v.reshape(ADAPTER_POOL * CAP, VALUE_WIDTH)[target]
        adapted_query_output = (base_product[:, :QUERY_WIDTH] + adapter_scale * query_rank_rows.astype(jnp.float32)).astype(jnp.bfloat16)
        adapted_value_output = (base_product[:, QUERY_WIDTH:] + adapter_scale * value_rank_rows.astype(jnp.float32)).astype(jnp.bfloat16)
        return (adapted_query_output, adapted_value_output)
    adapted_query_output, adapted_value_output = lax.map(one_block, (tokens.reshape(blocks, TOK_DEV, MODEL_WIDTH), slot_of.reshape(blocks, TOK_DEV)))
    return (adapted_query_output.reshape(TOKENS, QUERY_WIDTH), adapted_value_output.reshape(TOKENS, VALUE_WIDTH))
```

```python
import functools
import jax
import jax.numpy as jnp
from jax import lax
from jax.experimental import pallas as pl
from jax.experimental.pallas import tpu as pltpu
from jax.sharding import PartitionSpec as P

ADAPTER_SCALE = 0.5
DEVICE_CAP = 48
LINE = 4
BLOCK = LINE * DEVICE_CAP
BLOCKS = 2 * LINE
MIB = 1 << 20


def plan_kernel(coord_ref, ids_ref, row_ref, target_ref, count_ref):
    z, y, c = coord_ref[0], coord_ref[1], coord_ref[2]
    pool, toks = row_ref.shape[0], ids_ref.shape[1]
    catalog = lax.broadcasted_iota(jnp.int32, (pool, toks), 0)
    slot = jnp.sum(jnp.where(ids_ref[...] == catalog, row_ref[...], 0), axis=0, keepdims=True)
    chosen = (slot == catalog).astype(jnp.float32)
    chosen16 = chosen.astype(jnp.bfloat16)
    earlier = (
        lax.broadcasted_iota(jnp.int32, (toks, toks), 0) < lax.broadcasted_iota(jnp.int32, (toks, toks), 1)
    ).astype(jnp.float32).astype(jnp.bfloat16)
    before = jnp.dot(chosen16, earlier, preferred_element_type=jnp.float32)
    si = lax.broadcasted_iota(jnp.int32, (pool, pool), 0)
    sj = lax.broadcasted_iota(jnp.int32, (pool, pool), 1)
    lower = jnp.logical_and(lax.shift_right_logical(si, 2) == lax.shift_right_logical(sj, 2), sj < si)
    lower = lower.astype(jnp.float32).astype(jnp.bfloat16)
    offset = jnp.sum(jnp.dot(lower, chosen16, preferred_element_type=jnp.float32), axis=1, keepdims=True)
    rank = jnp.sum(chosen * (before + offset), axis=0, keepdims=True).astype(jnp.int32)
    owner = lax.shift_right_logical(slot, 2)
    owner_z = lax.shift_right_logical(owner, 3)
    owner_y = jnp.bitwise_and(lax.shift_right_logical(owner, 1), 3)
    owner_c = jnp.bitwise_and(owner, 1)
    dz = jnp.bitwise_and(owner_z - z + LINE, 3)
    dy = jnp.bitwise_and(owner_y - y + LINE, 3)
    step = jnp.where(owner_c == 0, dz, dy)
    sub = jnp.where(owner_c == 0, dy, dz)
    cross = jnp.bitwise_xor(owner_c, c)
    target_ref[...] = (cross * LINE + step) * BLOCK + sub * DEVICE_CAP + rank
    count_ref[...] = jnp.sum(chosen, axis=1, keepdims=True)


def plan(coords, ids, row):
    toks, pool = ids.shape[1], row.shape[0]
    return pl.pallas_call(
        plan_kernel,
        out_shape=(
            jax.ShapeDtypeStruct((1, toks), jnp.int32),
            jax.ShapeDtypeStruct((pool, 1), jnp.float32),
        ),
        in_specs=[
            pl.BlockSpec(memory_space=pltpu.SMEM),
            pl.BlockSpec(memory_space=pltpu.VMEM),
            pl.BlockSpec(memory_space=pltpu.VMEM),
        ],
        out_specs=(pl.BlockSpec(memory_space=pltpu.VMEM), pl.BlockSpec(memory_space=pltpu.VMEM)),
        compiler_params=pltpu.CompilerParams(vmem_limit_bytes=32 * MIB),
        name="plan",
    )(coords, ids, row)


def dispatch_kernel(target_ref, tokens_ref, gain_ref, normed_ref, *rest):
    blocks, (pick, factor) = rest[:BLOCKS], rest[BLOCKS:]
    k = pl.program_id(0)
    toks, feats = tokens_ref.shape
    chunk = normed_ref.shape[1]

    @pl.when(k == 0)
    def _():
        for b in range(BLOCKS):
            rows = lax.broadcasted_iota(jnp.int32, (BLOCK, toks), 0) + b * BLOCK
            pick[b] = (rows == target_ref[...]).astype(jnp.float32).astype(jnp.bfloat16)

        def sums(i, carry):
            part = tokens_ref[pl.ds(pl.multiple_of(i * 128, 128), 128), :].astype(jnp.float32)
            mean = jnp.sum(part * part, axis=1, keepdims=True) / feats
            factor[pl.ds(pl.multiple_of(i * 128, 128), 128), :] = lax.rsqrt(mean + 1e-06)
            return carry

        lax.fori_loop(0, toks // 128, sums, 0)

    cols = pl.ds(pl.multiple_of(k * chunk, 128), chunk)
    values = tokens_ref[:, cols].astype(jnp.float32)
    gain = gain_ref[:, cols].astype(jnp.float32)
    normed = (values * factor[...] * gain).astype(jnp.bfloat16)
    normed_ref[...] = normed
    for b in range(BLOCKS):
        blocks[b][...] = jnp.dot(pick[b], normed, preferred_element_type=jnp.float32).astype(jnp.bfloat16)


def dispatch(target, tokens, gain):
    toks, feats = tokens.shape
    chunk = 512
    return pl.pallas_call(
        dispatch_kernel,
        grid=(feats // chunk,),
        out_shape=(jax.ShapeDtypeStruct((toks, feats), jnp.bfloat16),)
        + (jax.ShapeDtypeStruct((BLOCK, feats), jnp.bfloat16),) * BLOCKS,
        in_specs=[
            pl.BlockSpec((1, toks), lambda k: (0, 0)),
            pl.BlockSpec((toks, feats), lambda k: (0, 0)),
            pl.BlockSpec((1, feats), lambda k: (0, 0)),
        ],
        out_specs=(pl.BlockSpec((toks, chunk), lambda k: (0, k)),)
        + (pl.BlockSpec((BLOCK, chunk), lambda k: (0, k)),) * BLOCKS,
        scratch_shapes=[
            pltpu.VMEM((BLOCKS, BLOCK, toks), jnp.bfloat16),
            pltpu.VMEM((toks, 1), jnp.float32),
        ],
        compiler_params=pltpu.CompilerParams(
            vmem_limit_bytes=48 * MIB, dimension_semantics=("arbitrary",)
        ),
        cost_estimate=pl.CostEstimate(flops=12 * 10**9, bytes_accessed=27 * 10**6, transcendentals=1024),
        name="dispatch",
    )(target, tokens, gain)


def adapter_kernel(aid_ref, *refs):
    xs, refs = refs[:BLOCKS], refs[BLOCKS:]
    downs, refs = refs[: 2 * LINE], refs[2 * LINE :]
    upqs, refs = refs[: 2 * LINE], refs[2 * LINE :]
    upvs, refs = refs[: 2 * LINE], refs[2 * LINE :]
    outs, refs = refs[:BLOCKS], refs[BLOCKS:]
    xbuf, dbuf, qbuf, vbuf, obuf, sem_x, sem_w, sem_o = refs
    rows = BLOCKS * DEVICE_CAP
    qcols, vcols = qbuf.shape[-1], vbuf.shape[-1]

    def x_copy(s, b):
        return pltpu.make_async_copy(
            xs[b].at[pl.ds(pl.multiple_of(s * DEVICE_CAP, DEVICE_CAP), DEVICE_CAP), :],
            xbuf.at[s, pl.ds(b * DEVICE_CAP, DEVICE_CAP), :],
            sem_x.at[s, b],
        )

    def o_copy(s, b):
        return pltpu.make_async_copy(
            obuf.at[s, pl.ds(b * DEVICE_CAP, DEVICE_CAP), :],
            outs[b].at[pl.ds(pl.multiple_of(s * DEVICE_CAP, DEVICE_CAP), DEVICE_CAP), :],
            sem_o.at[s, b],
        )

    def w_copies(s, ref):
        pairs = []
        for h in range(2):
            for i, (src, buf) in enumerate(((downs, dbuf), (upqs, qbuf), (upvs, vbuf))):
                at = src[2 * ref + h]
                at = at.at[pl.ds(2 * h, 2)] if at.shape[0] == 4 else at
                pairs.append(pltpu.make_async_copy(at, buf.at[s, pl.ds(2 * h, 2)], sem_w.at[s, 3 * h + i]))
        return pairs

    for s in range(LINE):
        for b in range(BLOCKS):
            x_copy(s, b).start()
        for copy in w_copies(s, s):
            copy.start()

    def one(s, carry):
        for b in range(BLOCKS):
            x_copy(s, b).wait()
        for copy in w_copies(s, 0):
            copy.wait()
        aid = aid_ref[s]
        x = xbuf[s]
        lane = lax.broadcasted_iota(jnp.int32, (rows, 128), 1)
        low = jnp.zeros((rows, 128), jnp.float32)
        for p in range(2):
            pair = jnp.concatenate([dbuf[s, 2 * p], dbuf[s, 2 * p + 1]], axis=1)
            wide = jnp.dot(x, pair, preferred_element_type=jnp.float32)
            low = jnp.where(aid == 2 * p, wide[:, :128], low)
            low = jnp.where(aid == 2 * p + 1, wide[:, 128:], low)
        turned = pltpu.roll(low, 64, 1)
        low_q = jnp.where(lane < 64, low, turned)
        low_v = jnp.where(lane < 64, turned, low)
        half = jnp.where(lane < 64, 0, 1)

        def spread(values):
            return jnp.concatenate(
                [jnp.where(aid == 2 * p + half, values, 0.0).astype(jnp.bfloat16) for p in range(2)], axis=1
            )

        up_q = qbuf[s].reshape(4 * 64, qcols)
        up_v = vbuf[s].reshape(4 * 64, vcols)
        obuf[s, :, :qcols] = jnp.dot(spread(low_q), up_q, preferred_element_type=jnp.float32).astype(jnp.bfloat16)
        obuf[s, :, qcols:] = jnp.dot(spread(low_v), up_v, preferred_element_type=jnp.float32).astype(jnp.bfloat16)
        for b in range(BLOCKS):
            o_copy(s, b).start()
        return carry

    lax.fori_loop(0, LINE, one, 0)
    for s in range(LINE):
        for b in range(BLOCKS):
            o_copy(s, b).wait()


def adapters(aid, xs, downs, upqs, upvs):
    feats = xs[0].shape[1]
    qcols, vcols = upqs[0].shape[-1], upvs[0].shape[-1]
    rows = BLOCKS * DEVICE_CAP
    anys = pl.BlockSpec(memory_space=pl.ANY)
    return pl.pallas_call(
        adapter_kernel,
        out_shape=(jax.ShapeDtypeStruct((BLOCK, qcols + vcols), jnp.bfloat16),) * BLOCKS,
        in_specs=[pl.BlockSpec(memory_space=pltpu.VMEM)] + [anys] * (BLOCKS + 6 * LINE),
        out_specs=(anys,) * BLOCKS,
        scratch_shapes=[
            pltpu.VMEM((LINE, rows, feats), jnp.bfloat16),
            pltpu.VMEM((LINE, 4, feats, 128), jnp.bfloat16),
            pltpu.VMEM((LINE, 4, 64, qcols), jnp.bfloat16),
            pltpu.VMEM((LINE, 4, 64, vcols), jnp.bfloat16),
            pltpu.VMEM((LINE, rows, qcols + vcols), jnp.bfloat16),
            pltpu.SemaphoreType.DMA((LINE, BLOCKS)),
            pltpu.SemaphoreType.DMA((LINE, 6)),
            pltpu.SemaphoreType.DMA((LINE, BLOCKS)),
        ],
        compiler_params=pltpu.CompilerParams(vmem_limit_bytes=56 * MIB),
        cost_estimate=pl.CostEstimate(flops=8 * 10**9, bytes_accessed=38 * 10**6, transcendentals=0),
        name="adapters",
    )(aid, *xs, *downs, *upqs, *upvs)


def combine_kernel(target_ref, base_ref, *refs):
    deltas, (q_ref, v_ref) = refs[:BLOCKS], refs[BLOCKS:]
    toks = target_ref.shape[0]
    total = None
    for b in range(BLOCKS):
        rows = lax.broadcasted_iota(jnp.int32, (toks, BLOCK), 1) + b * BLOCK
        pick = (rows == target_ref[...]).astype(jnp.float32).astype(jnp.bfloat16)
        part = jnp.dot(pick, deltas[b][...], preferred_element_type=jnp.float32)
        total = part if total is None else total + part
    result = (base_ref[...] + ADAPTER_SCALE * total).astype(jnp.bfloat16)
    qcols = q_ref.shape[1]
    q_ref[...] = result[:, :qcols]
    v_ref[...] = result[:, qcols:]


def combine(target, base, deltas, qcols):
    toks, cols = base.shape
    tile = 128
    return pl.pallas_call(
        combine_kernel,
        grid=(toks // tile,),
        out_shape=(
            jax.ShapeDtypeStruct((toks, qcols), jnp.bfloat16),
            jax.ShapeDtypeStruct((toks, cols - qcols), jnp.bfloat16),
        ),
        in_specs=[
            pl.BlockSpec((tile, 1), lambda i: (i, 0)),
            pl.BlockSpec((tile, cols), lambda i: (i, 0)),
        ]
        + [pl.BlockSpec((BLOCK, cols), lambda i: (0, 0))] * BLOCKS,
        out_specs=(
            pl.BlockSpec((tile, qcols), lambda i: (i, 0)),
            pl.BlockSpec((tile, cols - qcols), lambda i: (i, 0)),
        ),
        compiler_params=pltpu.CompilerParams(
            vmem_limit_bytes=48 * MIB, dimension_semantics=("arbitrary",)
        ),
        cost_estimate=pl.CostEstimate(flops=8 * 10**9, bytes_accessed=21 * 10**6, transcendentals=0),
        name="combine",
    )(target, base, *deltas)


def at(z, y, c):
    return (z % LINE) * 8 + (y % LINE) * 2 + c


def places():
    return [(z, y, c) for z in range(LINE) for y in range(LINE) for c in range(2)]


def row_pairs(cross, d):
    pairs = []
    for z, y, c in places():
        to = c ^ cross
        pairs.append((at(z, y, c), at(z + d, y, to) if to == 0 else at(z, y + d, to)))
    return pairs


def back(pairs):
    return [(j, i) for i, j in pairs]


def line_pairs(s):
    return [(at(z, y + s, c) if c == 0 else at(z + s, y, c), at(z, y, c)) for z, y, c in places()]


def gather_line(shard):
    half = shard.shape[0] // 2
    one = lax.ppermute(shard, "dev", line_pairs(1))
    three = lax.ppermute(shard, "dev", line_pairs(3))
    two_a = lax.ppermute(one[:half], "dev", line_pairs(1))
    two_b = lax.ppermute(three[half:], "dev", line_pairs(3))
    return [shard, shard, one, one, two_a, two_b, three, three]


def body(
    tokens,
    input_norm_gain,
    base_query_value_weight,
    adapter_down_weight,
    adapter_up_query,
    adapter_up_value,
    token_adapter_id,
    adapter_storage_row,
):
    toks = tokens.shape[0]
    pool = adapter_storage_row.shape[0]
    qcols = adapter_up_query.shape[2]
    me = lax.axis_index("dev")
    z, y, c = me // 8, (me // 2) % LINE, me % 2
    weight = lax.all_gather(base_query_value_weight, "grp", axis=0, tiled=True)
    downs = gather_line(adapter_down_weight)
    upqs = gather_line(adapter_up_query)
    upvs = gather_line(adapter_up_value)
    target, counts = plan(
        jnp.stack([z, y, c]).astype(jnp.int32), token_adapter_id.reshape(1, toks), adapter_storage_row.reshape(pool, 1)
    )
    everyone = lax.all_to_all(
        jnp.broadcast_to(counts.reshape(1, pool), (32, pool)), "dev", split_axis=0, concat_axis=0, tiled=True
    )
    normed, *rows = dispatch(target, tokens, input_norm_gain.reshape(1, -1))
    arrived = [
        rows[k * LINE + d] if (k, d) == (0, 0) else lax.ppermute(rows[k * LINE + d], "dev", row_pairs(k, d))
        for k in range(2)
        for d in range(LINE)
    ]
    cross = jnp.arange(BLOCKS) // LINE
    step = jnp.arange(BLOCKS) % LINE
    sender_c = jnp.bitwise_xor(c, cross)
    sender = jnp.where(
        c == 0,
        ((z - step) % LINE) * 8 + y * 2 + sender_c,
        z * 8 + ((y - step) % LINE) * 2 + sender_c,
    )
    sub = jnp.arange(LINE)
    owner = jnp.where(c == 0, z * 8 + ((y + sub) % LINE) * 2, ((z + sub) % LINE) * 8 + y * 2 + 1)
    slot = (owner[:, None] * 4 + jnp.arange(4)[None, :]).reshape(-1)
    pick_sender = (sender[:, None] == jnp.arange(32)[None, :]).astype(jnp.float32)
    pick_slot = (slot[:, None] == jnp.arange(pool)[None, :]).astype(jnp.float32)
    held = jnp.einsum("bd,dp,sp->sb", pick_sender, everyone, pick_slot).reshape(LINE, 4, BLOCKS)
    ends = jnp.stack([held[:, 0], held[:, 0] + held[:, 1], held[:, 0] + held[:, 1] + held[:, 2]], axis=1)
    aid = jnp.sum(
        (ends[..., None] <= jnp.arange(DEVICE_CAP, dtype=jnp.float32)).astype(jnp.int32), axis=1
    ).reshape(LINE, BLOCKS * DEVICE_CAP, 1)
    deltas = adapters(aid, arrived, downs, upqs, upvs)
    returned = [
        deltas[k * LINE + d]
        if (k, d) == (0, 0)
        else lax.ppermute(deltas[k * LINE + d], "dev", back(row_pairs(k, d)))
        for k in range(2)
        for d in range(LINE)
    ]
    base = jnp.dot(normed, weight, preferred_element_type=jnp.float32)
    return combine(target.reshape(toks, 1), base, returned, qcols)


def solution(mesh):
    in_specs = (
        P(("grp", "dev"), None),
        P(),
        P("grp", None),
        P("dev", None, None),
        P("dev", None, None),
        P("dev", None, None),
        P(("grp", "dev"), None),
        P(),
    )
    out_specs = (P(("grp", "dev"), None), P(("grp", "dev"), None))
    return jax.shard_map(body, mesh=mesh, in_specs=in_specs, out_specs=out_specs, check_vma=False)
```

```python
import functools
import jax
import jax.numpy as jnp
from jax import lax
from jax.experimental import pallas as pl
from jax.experimental.pallas import tpu as pltpu
from jax.sharding import PartitionSpec as P

ADAPTER_SCALE = 0.5
DEVICE_CAP = 48
LINE = 4
BLOCK = LINE * DEVICE_CAP
BLOCKS = 2 * LINE
PIECE = 64 // LINE
TAG = 128
MIB = 1 << 20


def plan_kernel(coord_ref, ids_ref, row_ref, target_ref, local_ref):
    z, y, c = coord_ref[0], coord_ref[1], coord_ref[2]
    pool, toks = row_ref.shape[0], ids_ref.shape[1]
    catalog = lax.broadcasted_iota(jnp.int32, (pool, toks), 0)
    slot = jnp.sum(jnp.where(ids_ref[...] == catalog, row_ref[...], 0), axis=0, keepdims=True)
    chosen = (slot == catalog).astype(jnp.float32)
    chosen16 = chosen.astype(jnp.bfloat16)
    earlier = (
        lax.broadcasted_iota(jnp.int32, (toks, toks), 0) < lax.broadcasted_iota(jnp.int32, (toks, toks), 1)
    ).astype(jnp.float32).astype(jnp.bfloat16)
    before = jnp.dot(chosen16, earlier, preferred_element_type=jnp.float32)
    si = lax.broadcasted_iota(jnp.int32, (pool, pool), 0)
    sj = lax.broadcasted_iota(jnp.int32, (pool, pool), 1)
    lower = jnp.logical_and(lax.shift_right_logical(si, 2) == lax.shift_right_logical(sj, 2), sj < si)
    lower = lower.astype(jnp.float32).astype(jnp.bfloat16)
    offset = jnp.sum(jnp.dot(lower, chosen16, preferred_element_type=jnp.float32), axis=1, keepdims=True)
    rank = jnp.sum(chosen * (before + offset), axis=0, keepdims=True).astype(jnp.int32)
    owner = lax.shift_right_logical(slot, 2)
    owner_z = lax.shift_right_logical(owner, 3)
    owner_y = jnp.bitwise_and(lax.shift_right_logical(owner, 1), 3)
    owner_c = jnp.bitwise_and(owner, 1)
    dz = jnp.bitwise_and(owner_z - z + LINE, 3)
    dy = jnp.bitwise_and(owner_y - y + LINE, 3)
    step = jnp.where(owner_c == 0, dz, dy)
    sub = jnp.where(owner_c == 0, dy, dz)
    cross = jnp.bitwise_xor(owner_c, c)
    target_ref[...] = (cross * LINE + step) * BLOCK + sub * DEVICE_CAP + rank
    local_ref[...] = jnp.bitwise_and(slot, 3).astype(jnp.float32)


def plan(coords, ids, row):
    toks = ids.shape[1]
    return pl.pallas_call(
        plan_kernel,
        out_shape=(
            jax.ShapeDtypeStruct((1, toks), jnp.int32),
            jax.ShapeDtypeStruct((1, toks), jnp.float32),
        ),
        in_specs=[
            pl.BlockSpec(memory_space=pltpu.SMEM),
            pl.BlockSpec(memory_space=pltpu.VMEM),
            pl.BlockSpec(memory_space=pltpu.VMEM),
        ],
        out_specs=(pl.BlockSpec(memory_space=pltpu.VMEM), pl.BlockSpec(memory_space=pltpu.VMEM)),
        compiler_params=pltpu.CompilerParams(vmem_limit_bytes=32 * MIB),
        name="plan",
    )(coords, ids, row)


def dispatch_kernel(target_ref, local_ref, tokens_ref, gain_ref, normed_ref, *rest):
    blocks, (pick, factor, held, sem) = rest[:BLOCKS], rest[BLOCKS:]
    k = pl.program_id(0)
    toks, feats = tokens_ref.shape
    chunk = normed_ref.shape[1]
    last = pl.ds(feats, TAG)

    def copies(cols, step):
        return [
            pltpu.make_async_copy(held.at[pl.ds(b * BLOCK, BLOCK), cols], blocks[b].at[:, cols], sem.at[step, b])
            for b in range(BLOCKS)
        ]

    def columns(step):
        return pl.ds(pl.multiple_of(step * chunk, 128), chunk)

    @pl.when(k == 0)
    def _():
        tags = jnp.broadcast_to(local_ref[...], (TAG, toks)).astype(jnp.bfloat16)
        for b in range(BLOCKS):
            rows = lax.broadcasted_iota(jnp.int32, (BLOCK, toks), 0) + b * BLOCK
            here = (rows == target_ref[...]).astype(jnp.float32).astype(jnp.bfloat16)
            pick[b * BLOCK : (b + 1) * BLOCK, :] = here
            tag = lax.dot_general(here, tags, (((1,), (1,)), ((), ())), preferred_element_type=jnp.float32)
            held[b * BLOCK : (b + 1) * BLOCK, feats:] = tag.astype(jnp.bfloat16)
        for copy in copies(last, feats // chunk):
            copy.start()

        def sums(i, carry):
            part = tokens_ref[pl.ds(pl.multiple_of(i * 128, 128), 128), :].astype(jnp.float32)
            mean = jnp.sum(part * part, axis=1, keepdims=True) / feats
            factor[pl.ds(pl.multiple_of(i * 128, 128), 128), :] = lax.rsqrt(mean + 1e-06)
            return carry

        lax.fori_loop(0, toks // 128, sums, 0)

    cols = columns(k)
    values = tokens_ref[:, cols].astype(jnp.float32)
    gain = gain_ref[:, cols].astype(jnp.float32)
    normed = (values * factor[...] * gain).astype(jnp.bfloat16)
    normed_ref[...] = normed
    held[:, cols] = jnp.dot(pick[...], normed, preferred_element_type=jnp.float32).astype(jnp.bfloat16)
    for copy in copies(cols, k):
        copy.start()

    @pl.when(k == pl.num_programs(0) - 1)
    def _():
        for step in range(feats // chunk):
            for copy in copies(columns(step), step):
                copy.wait()
        for copy in copies(last, feats // chunk):
            copy.wait()


def dispatch(target, local, tokens, gain):
    toks, feats = tokens.shape
    chunk = 512
    return pl.pallas_call(
        dispatch_kernel,
        grid=(feats // chunk,),
        out_shape=(jax.ShapeDtypeStruct((toks, feats), jnp.bfloat16),)
        + (jax.ShapeDtypeStruct((BLOCK, feats + TAG), jnp.bfloat16),) * BLOCKS,
        in_specs=[
            pl.BlockSpec((1, toks), lambda k: (0, 0)),
            pl.BlockSpec((1, toks), lambda k: (0, 0)),
            pl.BlockSpec((toks, feats), lambda k: (0, 0)),
            pl.BlockSpec((1, feats), lambda k: (0, 0)),
        ],
        out_specs=(pl.BlockSpec((toks, chunk), lambda k: (0, k)),) + (pl.BlockSpec(memory_space=pl.ANY),) * BLOCKS,
        scratch_shapes=[
            pltpu.VMEM((BLOCKS * BLOCK, toks), jnp.bfloat16),
            pltpu.VMEM((toks, 1), jnp.float32),
            pltpu.VMEM((BLOCKS * BLOCK, feats + TAG), jnp.bfloat16),
            pltpu.SemaphoreType.DMA((feats // chunk + 1, BLOCKS)),
        ],
        compiler_params=pltpu.CompilerParams(
            vmem_limit_bytes=56 * MIB, dimension_semantics=("arbitrary",)
        ),
        cost_estimate=pl.CostEstimate(flops=12 * 10**9, bytes_accessed=27 * 10**6, transcendentals=1024),
        name="dispatch",
    )(target, local, tokens, gain)


def adapter_kernel(qcols, count, *refs):
    xs, refs = refs[:count], refs[count:]
    downs, refs = refs[: 2 * LINE], refs[2 * LINE :]
    up_own, up_far, refs = refs[0], refs[1], refs[2:]
    outs, refs = refs[:count], refs[count:]
    xbuf, dbuf, ubuf, obuf, sem_x, sem_w, sem_o = refs
    rows = count * DEVICE_CAP

    def x_copy(s, b):
        return pltpu.make_async_copy(
            xs[b].at[pl.ds(pl.multiple_of(s * DEVICE_CAP, DEVICE_CAP), DEVICE_CAP), :],
            xbuf.at[s, pl.ds(b * DEVICE_CAP, DEVICE_CAP), :],
            sem_x.at[s, b],
        )

    def o_copy(s, b):
        return pltpu.make_async_copy(
            obuf.at[s, pl.ds(b * DEVICE_CAP, DEVICE_CAP), :],
            outs[b].at[pl.ds(pl.multiple_of(s * DEVICE_CAP, DEVICE_CAP), DEVICE_CAP), :],
            sem_o.at[s, b],
        )

    def w_copies(s, ref):
        pairs = []
        for p in range(LINE):
            part = pl.ds(p * PIECE, PIECE)
            src = up_own.at[:, part, :] if ref == 0 else up_far.at[p, ref - 1]
            pairs.append(pltpu.make_async_copy(src, ubuf.at[s, :, part, :], sem_w.at[s, 2 + p]))
        for h in range(2):
            src = downs[2 * ref + h]
            src = src.at[pl.ds(2 * h, 2)] if src.shape[0] == 4 else src
            pairs.append(pltpu.make_async_copy(src, dbuf.at[s, pl.ds(2 * h, 2)], sem_w.at[s, h]))
        return pairs

    for s in range(LINE):
        for b in range(count):
            x_copy(s, b).start()
        for copy in w_copies(s, s):
            copy.start()

    def one(s, carry):
        for b in range(count):
            x_copy(s, b).wait()
        for copy in w_copies(s, 0):
            copy.wait()
        x = xbuf[s, :, : dbuf.shape[2]]
        aid = xbuf[s, :, dbuf.shape[2] :].astype(jnp.float32)
        lane = lax.broadcasted_iota(jnp.int32, (rows, 128), 1)
        low = jnp.zeros((rows, 128), jnp.float32)
        for p in range(2):
            pair = jnp.concatenate([dbuf[s, 2 * p], dbuf[s, 2 * p + 1]], axis=1)
            wide = jnp.dot(x, pair, preferred_element_type=jnp.float32)
            low = jnp.where(aid == 2 * p, wide[:, :128], low)
            low = jnp.where(aid == 2 * p + 1, wide[:, 128:], low)
        turned = pltpu.roll(low, 64, 1)
        low_q = jnp.where(lane < 64, low, turned)
        low_v = jnp.where(lane < 64, turned, low)
        half = jnp.where(lane < 64, 0.0, 1.0)

        def spread(values):
            return jnp.concatenate(
                [jnp.where(aid == 2 * p + half, values, 0.0).astype(jnp.bfloat16) for p in range(2)], axis=1
            )

        up = ubuf[s].reshape(4 * 64, ubuf.shape[-1])
        up_q, up_v = up[:, :qcols], up[:, qcols:]
        obuf[s, :, :qcols] = jnp.dot(spread(low_q), up_q, preferred_element_type=jnp.float32).astype(jnp.bfloat16)
        obuf[s, :, qcols:] = jnp.dot(spread(low_v), up_v, preferred_element_type=jnp.float32).astype(jnp.bfloat16)
        for b in range(count):
            o_copy(s, b).start()
        return carry

    lax.fori_loop(0, LINE, one, 0)
    for s in range(LINE):
        for b in range(count):
            o_copy(s, b).wait()


def adapters(xs, downs, up_own, up_far, qcols):
    feats = downs[0].shape[1]
    cols = up_own.shape[-1]
    count = len(xs)
    rows = count * DEVICE_CAP
    anys = pl.BlockSpec(memory_space=pl.ANY)
    return pl.pallas_call(
        functools.partial(adapter_kernel, qcols, count),
        out_shape=(jax.ShapeDtypeStruct((BLOCK, cols), jnp.bfloat16),) * count,
        in_specs=[anys] * (count + 2 * LINE + 2),
        out_specs=(anys,) * count,
        scratch_shapes=[
            pltpu.VMEM((LINE, rows, feats + TAG), jnp.bfloat16),
            pltpu.VMEM((LINE, 4, feats, 128), jnp.bfloat16),
            pltpu.VMEM((LINE, 4, 64, cols), jnp.bfloat16),
            pltpu.VMEM((LINE, rows, cols), jnp.bfloat16),
            pltpu.SemaphoreType.DMA((LINE, count)),
            pltpu.SemaphoreType.DMA((LINE, 6)),
            pltpu.SemaphoreType.DMA((LINE, count)),
        ],
        compiler_params=pltpu.CompilerParams(vmem_limit_bytes=56 * MIB),
        cost_estimate=pl.CostEstimate(flops=4 * 10**9, bytes_accessed=29 * 10**6, transcendentals=0),
        name="adapters",
    )(*xs, *downs, up_own, up_far)


def combine_kernel(coord_ref, target_ref, mine_ref, theirs_ref, *refs):
    deltas, (q_ref, v_ref, held, sem) = refs[:BLOCKS], refs[BLOCKS:]
    toks, rows = target_ref.shape[0], BLOCKS * BLOCK

    @pl.when(pl.program_id(0) == 0)
    def _():
        copies = [
            pltpu.make_async_copy(deltas[b], held.at[pl.ds(b * BLOCK, BLOCK), :], sem.at[b]) for b in range(BLOCKS)
        ]
        for copy in copies:
            copy.start()
        for copy in copies:
            copy.wait()

    row = lax.broadcasted_iota(jnp.int32, (toks, rows), 1)
    pick = (row == target_ref[...]).astype(jnp.float32).astype(jnp.bfloat16)
    total = jnp.dot(pick, held[...], preferred_element_type=jnp.float32)
    first = coord_ref[2] == 0
    low = jnp.where(first, mine_ref[...], theirs_ref[...])
    high = jnp.where(first, theirs_ref[...], mine_ref[...])
    half, qcols = low.shape[1], q_ref.shape[1]
    low = (low + ADAPTER_SCALE * total[:, :half]).astype(jnp.bfloat16)
    high = (high + ADAPTER_SCALE * total[:, half:]).astype(jnp.bfloat16)
    q_ref[:, :half] = low
    q_ref[:, half:] = high[:, : qcols - half]
    v_ref[...] = high[:, qcols - half :]


def combine(coords, target, mine, theirs, deltas, qcols):
    toks, half = mine.shape
    cols = 2 * half
    tile = 512
    return pl.pallas_call(
        combine_kernel,
        grid=(toks // tile,),
        out_shape=(
            jax.ShapeDtypeStruct((toks, qcols), jnp.bfloat16),
            jax.ShapeDtypeStruct((toks, cols - qcols), jnp.bfloat16),
        ),
        in_specs=[
            pl.BlockSpec(memory_space=pltpu.SMEM),
            pl.BlockSpec((tile, 1), lambda i: (i, 0)),
            pl.BlockSpec((tile, half), lambda i: (i, 0)),
            pl.BlockSpec((tile, half), lambda i: (i, 0)),
        ]
        + [pl.BlockSpec(memory_space=pl.ANY)] * BLOCKS,
        out_specs=(
            pl.BlockSpec((tile, qcols), lambda i: (i, 0)),
            pl.BlockSpec((tile, cols - qcols), lambda i: (i, 0)),
        ),
        scratch_shapes=[
            pltpu.VMEM((BLOCKS * BLOCK, cols), jnp.bfloat16),
            pltpu.SemaphoreType.DMA((BLOCKS,)),
        ],
        compiler_params=pltpu.CompilerParams(
            vmem_limit_bytes=48 * MIB, dimension_semantics=("arbitrary",)
        ),
        cost_estimate=pl.CostEstimate(flops=8 * 10**9, bytes_accessed=21 * 10**6, transcendentals=0),
        name="combine",
    )(coords, target, mine, theirs, *deltas)


def at(z, y, c):
    return (z % LINE) * 8 + (y % LINE) * 2 + c


def places():
    return [(z, y, c) for z in range(LINE) for y in range(LINE) for c in range(2)]


def row_pairs(cross, d):
    pairs = []
    for z, y, c in places():
        to = c ^ cross
        pairs.append((at(z, y, c), at(z + d, y, to) if to == 0 else at(z, y + d, to)))
    return pairs


def back(pairs):
    return [(j, i) for i, j in pairs]


def line_pairs(s):
    return [(at(z, y + s, c) if c == 0 else at(z + s, y, c), at(z, y, c)) for z, y, c in places()]


def line(shard, s):
    return lax.ppermute(shard, "dev", line_pairs(s))


def body(
    tokens,
    input_norm_gain,
    base_query_value_weight,
    adapter_down_weight,
    adapter_up_query,
    adapter_up_value,
    token_adapter_id,
    adapter_storage_row,
):
    toks = tokens.shape[0]
    pool = adapter_storage_row.shape[0]
    qcols = adapter_up_query.shape[2]
    me = lax.axis_index("dev")
    z, y, c = me // 8, (me // 2) % LINE, me % 2
    coords = jnp.stack([z, y, c]).astype(jnp.int32)
    half = adapter_down_weight.shape[0] // 2
    one, three = line(adapter_down_weight, 1), line(adapter_down_weight, 3)
    up = jnp.concatenate([adapter_up_query, adapter_up_value], axis=2)
    piece = lax.dynamic_slice_in_dim(up, lax.axis_index("grp") * PIECE, PIECE, axis=1)
    pieces = jnp.stack([line(piece, s) for s in range(1, LINE)])
    up_far = lax.all_gather(pieces, "grp", axis=0)
    target, local = plan(coords, token_adapter_id.reshape(1, toks), adapter_storage_row.reshape(pool, 1))
    normed, *rows = dispatch(target, local, tokens, input_norm_gain.reshape(1, -1))
    own, other = rows[:LINE], rows[LINE:]
    other[0] = lax.ppermute(other[0], "dev", row_pairs(1, 0))
    own = [own[0]] + [lax.ppermute(own[d], "dev", row_pairs(0, d)) for d in range(1, LINE)]
    one, three, other[0] = lax.optimization_barrier((one, three, other[0]))
    two_a, two_b = line(one[:half], 1), line(three[half:], 3)
    width = base_query_value_weight.shape[1] // 2
    weight = lax.dynamic_slice_in_dim(base_query_value_weight, c * width, width, axis=1)
    other, own[1], weight, up_far = lax.optimization_barrier((other, own[1], weight, up_far))
    mine = lax.all_gather(weight, "grp", axis=0, tiled=True)
    other = [other[0]] + [lax.ppermute(other[d], "dev", row_pairs(1, d)) for d in range(1, LINE)]
    downs = [adapter_down_weight, adapter_down_weight, one, one, two_a, two_b, three, three]
    own = adapters(own, downs, up, up_far, qcols)
    other, _ = lax.optimization_barrier((other, own))
    own = [own[0]] + [lax.ppermute(own[d], "dev", back(row_pairs(0, d))) for d in range(1, LINE)]
    other = adapters(other, downs, up, up_far, qcols)
    other, own[1], own[3], mine = lax.optimization_barrier((list(other), own[1], own[3], mine))
    other = [lax.ppermute(other[d], "dev", back(row_pairs(1, d))) for d in range(LINE)]
    theirs = lax.ppermute(mine, "dev", [(i, i ^ 1) for i in range(32)])
    mine = jnp.dot(normed, mine, preferred_element_type=jnp.float32)
    theirs = jnp.dot(normed, theirs, preferred_element_type=jnp.float32)
    return combine(coords, target.reshape(toks, 1), mine, theirs, own + other, qcols)


def solution(mesh):
    in_specs = (
        P(("grp", "dev"), None),
        P(),
        P("grp", None),
        P("dev", None, None),
        P("dev", None, None),
        P("dev", None, None),
        P(("grp", "dev"), None),
        P(),
    )
    out_specs = (P(("grp", "dev"), None), P(("grp", "dev"), None))
    return jax.shard_map(body, mesh=mesh, in_specs=in_specs, out_specs=out_specs, check_vma=False)
```
